32 devices in a mesh: dp: 4 (over z), tensor: 8 (over y, x, core).
Axes of the slice: x: 2, y: 2, z: 4, core: 2. Of those that a mesh axis runs over, the one named last changes fastest.
Arguments:
- hidden: bfloat16 [3584, 4096], P('dp', 'tensor')
- gain: bfloat16 [4096], P('tensor'), may hold values from 0.5 to 1.5
- head_weight: bfloat16 [4096, 32000], P('dp', 'tensor')
- targets: int32 [3584], P('dp'), may hold values from 0 to 31999
- seq_ids: int32 [3584], P(('dp', 'tensor')), may hold values from 0 to 15, never falling along the last dimension, each value on 1 to 1792 neighbouring positions
- live: int32 [3584], P(('dp', 'tensor')), may hold values 0 or 1
Outputs:
- logprob: float32 [3584], P(('dp', 'tensor'))
- entropy: float32 [3584], P(('dp', 'tensor'))
- seq_mean: float32 [16], replicated
The draws below stay inside these ranges and needn't reach their ends.
Inputs may be any that keep to these rules, and one draw needn't show every extreme that they name: `seq_ids`: sequence numbers never fall along the tokens; each sequence has 1 to 1792 tokens, one exactly 1792.
All inputs are finite; a program needn't handle non-finite values. No bound on the sum of `live` on one device may be relied on, other than what follows from the above.
Results may differ from the reference program's by a relative error of at most 0.0015.
Values may be sent and summed in bfloat16 or wider, within the bound.
A program may use at most 128 MiB of HBM per device.

```python
import math
import jax
import jax.numpy as jnp
import numpy as np
from jax import lax

D = 4096
V = 32000
TOKENS = 3584
SEQS = 16
LONGEST = 1792


def column_of(key, index):
    return jax.random.normal(jax.random.fold_in(key, index), (D,), jnp.float32) * 3.0 / math.sqrt(D)


def column_table(key, indices):

    def single(index):
        return column_of(key, index)
    return jax.vmap(single)(indices)


def draw_head_weight(key, part):
    weight_key = jax.random.fold_in(key, 13)
    full = column_table(weight_key, jnp.arange(V)).T
    return full.astype(jnp.bfloat16)


def draw_hidden(key, part):
    row_key = jax.random.fold_in(key, 14)
    row_scale = jnp.exp(jax.random.uniform(jax.random.fold_in(key, 15), (TOKENS, 1), jnp.float32, 0.0, math.log(10.0)))
    col_scale = jnp.exp(jax.random.uniform(jax.random.fold_in(key, 16), (1, D), jnp.float32, 0.0, math.log(10.0)))
    base = jax.random.normal(row_key, (TOKENS, D), jnp.float32)
    values = base * row_scale * col_scale
    return values.astype(jnp.bfloat16)


def plant(entries, rng, low, top_value):
    longest = entries.shape.index(max(entries.shape))
    spots = []
    for shift in (0, 1):
        where = [jax.random.randint(jax.random.fold_in(rng, axis), (), 0, length) for axis, length in enumerate(entries.shape)]
        where[longest] = (where[longest] + shift) % entries.shape[longest]
        spots.append(tuple(where))
    return entries.at[spots[0]].set(low).at[spots[1]].set(top_value)


def rank_table(number_of, slope):
    loads = [(1 << 20) // math.isqrt(grade ** slope) + 1 for grade in range(1, number_of + 1)]
    scale = 1 + sum(loads) // (1 << 30)
    return np.cumsum(np.array([max(1, weight // scale) for weight in loads]))


def ranked(key, dims, number_of, lean):
    listing = rank_table(number_of, lean)
    pick = jax.random.randint(jax.random.fold_in(key, 1), dims, 0, int(listing[number_of - 1]))
    grade = jnp.searchsorted(jnp.asarray(listing, jnp.int32), pick, side="right")
    return jax.random.permutation(jax.random.fold_in(key, 2), number_of)[grade].astype(jnp.int32)


def profile(amount, total, bound, slope):
    loads = [(1 << 20) // math.isqrt(standing ** slope) + 1 for standing in range(2, amount + 1)]
    surplus, given = total - bound - (amount - 1), [1] * (amount - 1)
    while surplus > 0:
        free = [i for i in range(amount - 1) if given[i] < bound]
        mass, left = sum([loads[i] for i in free]), surplus
        for i in free:
            addition = min(bound - given[i], max(1, left * loads[i] // mass), surplus)
            given[i] = given[i] + addition
            surplus = surplus - addition
    return np.array([bound] + given)


def ragged_sizes(stream_key, amount, total, bound, skew):
    if amount == 2:
        one = jax.random.randint(stream_key, (), max(1, total - bound), min(bound, total - 1) + 1)
        return jnp.stack([one, total - one])
    sizes = jnp.asarray(profile(amount, total, bound, skew), jnp.int32)
    pairs = (amount - 1) // 2
    giver, receiver = sizes[1:1 + 2 * pairs:2], sizes[2:2 + 2 * pairs:2]
    slack = jnp.minimum(giver - 1, bound - receiver)
    moved = jax.random.randint(jax.random.fold_in(stream_key, 1), (pairs,), 0, 1 << 20) % (slack + 1)
    sizes = sizes.at[1:1 + 2 * pairs:2].set(giver - moved).at[2:2 + 2 * pairs:2].set(receiver + moved)
    return sizes[jax.random.permutation(jax.random.fold_in(stream_key, 2), amount)]


def setup_inputs(seed: int = 0) -> dict:
    keys = jax.random.split(jax.random.key(seed), 7)
    hidden = draw_hidden(jax.random.fold_in(keys[6], 71), 0)
    gain = jnp.clip(1.0 + 0.1 * jax.random.normal(keys[1], (D,), jnp.float32), 0.5, 1.5).astype(jnp.bfloat16)
    head_weight = draw_head_weight(jax.random.fold_in(keys[6], 71), 0)
    targets = plant(ranked(keys[3], (TOKENS,), V, 2), jax.random.fold_in(keys[3], 3), 0, V - 1).astype(jnp.int32)
    seq_ids = jnp.searchsorted(jnp.cumsum(ragged_sizes(keys[4], SEQS, TOKENS, LONGEST, 2)), jnp.arange(TOKENS), side="right").astype(jnp.int32)
    live = plant((jax.random.randint(keys[5], (TOKENS,), 0, 8) < 7).astype(jnp.int32), jax.random.fold_in(keys[5], 1), 0, 1)
    return dict(hidden=hidden, gain=gain, head_weight=head_weight, targets=targets, seq_ids=seq_ids, live=live)


def reference(hidden, gain, head_weight, targets, seq_ids, live):
    values = hidden.astype(jnp.float32)
    meansq = lax.optimization_barrier(jnp.mean(values * values, axis=-1, keepdims=True))
    normed = (values * lax.rsqrt(meansq + 1e-05) * gain.astype(jnp.float32)).astype(jnp.bfloat16)
    width = min(512, TOKENS)
    blocks = normed.reshape(TOKENS // width, width, D)
    chosen = targets.reshape(TOKENS // width, width)

    def one_block(pair):
        rows, picks = pair
        scores = jnp.dot(rows, head_weight, preferred_element_type=jnp.float32)
        top = lax.optimization_barrier(jnp.max(scores, axis=-1, keepdims=True))
        shifted = scores - top
        expo = jnp.exp(shifted)
        total = lax.optimization_barrier(jnp.sum(expo, axis=-1))
        spread = lax.optimization_barrier(jnp.sum(expo * shifted, axis=-1))
        target_score = jnp.take_along_axis(scores, picks[:, None], axis=1)[:, 0]
        logp = target_score - top[:, 0] - jnp.log(total)
        entro = jnp.log(total) - spread / total
        return (logp, entro)
    logp, entro = lax.map(one_block, (blocks, chosen))
    weight = live.astype(jnp.float32)
    logprob = logp.reshape(TOKENS) * weight
    entropy = entro.reshape(TOKENS) * weight
    sums = jax.ops.segment_sum(logprob, seq_ids, num_segments=SEQS)
    counts = jax.ops.segment_sum(weight, seq_ids, num_segments=SEQS)
    seq_mean = sums / jnp.maximum(counts, 1.0)
    return (logprob, entropy, seq_mean)
```

```python
import functools

import jax
import jax.numpy as jnp
from jax import lax
from jax.experimental import pallas as pl
from jax.experimental.pallas import tpu as pltpu
from jax.sharding import PartitionSpec as P

SEQ_DEV = 4
GROUP = 4
MESH = pl.DeviceIdType.MESH


def window(vocab_dev, group):
    part = vocab_dev // group
    for align in (16, 8):
        starts = [part * p // align * align for p in range(group)]
        need = max(part * (p + 1) - s for p, s in enumerate(starts))
        length = -(-need // align) * align
        if all(s + length <= vocab_dev for s in starts):
            return part, align, length
    raise ValueError("shard")


def pieces(length, align, many):
    units = length // align
    sizes = [(units // many + (i < units % many)) * align for i in range(many)]
    out, at = [], 0
    for s in sizes:
        out.append((at, s))
        at += s
    return out


def kernel(
    cfg,
    hid, gain, wt, targets, seq_ids, live,
    logprob, entropy, seq_mean,
    x, w, tgt, sq_out, sq_in, st, st_out, st_in, sq_seq_out, sq_seq_in,
    w_send, w_recv, w_loc, z_send, z_recv, p_send, p_recv, s_send, s_recv, g_send, g_recv, m_send, m_recv,
):
    (dp, tn, g, part, align, length, chunks, tile) = cfg
    z, t = lax.axis_index("dp"), lax.axis_index("tensor")
    p = lax.rem(z, g)
    zb = z - p
    R, Dl = hid.shape
    Kl = wt.shape[1]
    chips = tn // 2
    N = dp * tn
    me = z * tn + t
    share = R // tn
    seqs = seq_mean.shape[0]

    def remote(src, dst, ss, rs, zz, tt):
        return pltpu.make_async_remote_copy(
            src_ref=src, dst_ref=dst, send_sem=ss, recv_sem=rs,
            device_id={"dp": zz, "tensor": tt}, device_id_type=MESH,
        )

    barrier = pltpu.get_barrier_semaphore()

    @pl.loop(1, N)
    def _(d):
        o = lax.rem(me + d, N)
        pl.semaphore_signal(
            barrier, inc=1, device_id={"dp": o // tn, "tensor": lax.rem(o, tn)}, device_id_type=MESH
        )

    pl.semaphore_wait(barrier, N - 1)

    def start_of(pp):
        return pl.multiple_of(part * pp // align * align, align)

    def w_copy(d, c, to, frm):
        off, size = chunks[c]
        return remote(
            wt.at[pl.ds(start_of(lax.rem(to, g)) + off, size)],
            w.at[pl.ds(off, size), pl.ds(pl.multiple_of(frm * Kl, Kl), Kl)],
            w_send.at[d - 1, c], w_recv.at[d - 1, c], to, t,
        )

    def w_own(c):
        off, size = chunks[c]
        return pltpu.make_async_copy(
            wt.at[pl.ds(start_of(p) + off, size)],
            w.at[pl.ds(off, size), pl.ds(pl.multiple_of(z * Kl, Kl), Kl)],
            w_loc.at[c],
        )

    def start_w(c):
        for d in range(1, dp):
            w_copy(d, c, lax.rem(z + d, dp), z).start()
        w_own(c).start()

    values = hid[...].astype(jnp.float32)
    sums = jnp.sum(values * values, axis=-1, keepdims=True)
    sq_out[...] = jnp.transpose(jnp.broadcast_to(sums, (R, 128)))[:8, :]

    def sq_copy(d, slot):
        return remote(sq_out, sq_in.at[slot], m_send.at[0], m_recv.at[0], z, lax.rem(t + d, tn))

    @pl.loop(1, tn)
    def _(d):
        sq_copy(d, t).start()

    sq_in[t] = sq_out[...]

    def tgt_copy(d, slot):
        return remote(
            targets, tgt.at[slot], g_send.at[d - 1], g_recv.at[d - 1], zb + lax.rem(p + d, g), t
        )

    for d in range(1, g):
        tgt_copy(d, p).start()
    tgt[p] = targets[...]
    for c in range(len(chunks)):
        start_w(c)

    pltpu.make_async_copy(
        sq_in.at[pl.ds(0, tn - 1)], sq_in.at[pl.ds(0, tn - 1)], m_recv.at[0]
    ).wait()
    square = jnp.sum(sq_in[...], axis=0)
    wide = jnp.transpose(jnp.concatenate([square] * 16, axis=0))
    scale = lax.rsqrt(wide / (tn * Dl) + 1e-05)
    rows0 = pl.ds(pl.multiple_of(p * R, R), R)
    for i in range(Dl // 128):
        cut = slice(i * 128, (i + 1) * 128)
        x[rows0, pl.ds(pl.multiple_of(t * Dl + i * 128, 128), 128)] = (
            values[:, cut] * scale * gain[:, cut].astype(jnp.float32)
        ).astype(jnp.bfloat16)

    def block(k, tt):
        return x.at[pl.ds(pl.multiple_of(k * R, R), R), pl.ds(pl.multiple_of(tt * Dl, Dl), Dl)]

    def z_copy(k, way):
        step = 1 if way == 0 else -1
        return remote(block(k, t), block(k, t), z_send.at[way, k], z_recv.at[k], z + step, t)

    def p_copy(k, j, src):
        return remote(
            block(k, src), block(k, src), p_send.at[k, j - 1], p_recv.at[k, j - 1], z, t ^ (2 * j)
        )

    def s_copy(k, j, src):
        return remote(block(k, src), block(k, src), s_send.at[k, j], s_recv.at[k, j], z, t ^ 1)

    def spread_out(k):
        for j in range(1, chips):
            p_copy(k, j, t).start()
        s_copy(k, 0, t).start()

    def gather_in(k):
        for j in range(1, chips):
            p_copy(k, j, t ^ (2 * j)).wait_recv()
            s_copy(k, j, t ^ (2 * j)).start()

    def each(s, fn):
        if s == 0:
            fn(p, None)
            return

        @pl.when(p - s >= 0)
        def _():
            fn(p - s, 0)

        @pl.when(p + s < g)
        def _():
            fn(p + s, 1)

    def arrive(k, way):
        if way is not None:
            z_copy(k, way).wait_recv()
        if way in (None, 0):

            @pl.when(p < g - 1)
            def _():
                z_copy(k, 0).start()

        if way in (None, 1):

            @pl.when(p > 0)
            def _():
                z_copy(k, 1).start()

        spread_out(k)

    each(0, arrive)
    for s in range(1, g):
        each(s, arrive)
        each(s - 1, lambda k, way: gather_in(k))
    each(g - 1, lambda k, way: gather_in(k))

    @pl.loop(0, g)
    def _(k):
        for j in range(chips):
            s_copy(k, j, t ^ 1 ^ (2 * j)).wait_recv()

    for d in range(1, g):
        tgt_copy(d, lax.rem(p - d + g, g)).wait_recv()

    first = t * (g * part) + start_of(p)
    low = p * part - start_of(p)
    for c, (off, size) in enumerate(chunks):
        w_own(c).wait()
        for d in range(1, dp):
            w_copy(d, c, z, lax.rem(z - d + dp, dp)).wait_recv()

        @pl.loop(0, R // tile * g)
        def _(b):
            k = b // (R // tile)
            lane = pl.multiple_of(lax.rem(b, R // tile) * tile, tile)
            scores = lax.dot_general(
                w[pl.ds(off, size), :],
                x[pl.ds(pl.multiple_of(b * tile, tile), tile), :],
                (((1,), (1,)), ((), ())),
                preferred_element_type=jnp.float32,
            )
            row = lax.broadcasted_iota(jnp.int32, (size, 1), 0) + off
            edge = c in (0, len(chunks) - 1)
            if edge:
                inside = (row >= low) & (row < low + part)
                top = jnp.max(jnp.where(inside, scores, -jnp.inf), axis=0, keepdims=True)
            else:
                top = jnp.max(scores, axis=0, keepdims=True)
            local = tgt[k, :, pl.ds(lane, tile)] - first
            local = jnp.where((local >= low) & (local < low + part), local, -1)
            picked = jnp.sum(jnp.where(row == local, scores, 0.0), axis=0, keepdims=True)
            if c > 0:
                was = st[k, 0:1, pl.ds(lane, tile)]
                top = jnp.maximum(top, was)
            shifted = scores - top
            if edge:
                shifted = jnp.where(inside, shifted, -1e4)
            expo = jnp.exp(shifted)
            total = jnp.sum(expo, axis=0, keepdims=True)
            spread = jnp.sum(expo * shifted, axis=0, keepdims=True)
            if c > 0:
                fall = was - top
                by = jnp.exp(fall)
                t0 = st[k, 1:2, pl.ds(lane, tile)]
                total += t0 * by
                spread += (st[k, 2:3, pl.ds(lane, tile)] + fall * t0) * by
                picked += st[k, 3:4, pl.ds(lane, tile)]
            st[k, 0:1, pl.ds(lane, tile)] = top
            st[k, 1:2, pl.ds(lane, tile)] = total
            st[k, 2:3, pl.ds(lane, tile)] = spread
            st[k, 3:4, pl.ds(lane, tile)] = picked

    n = g * tn
    mine = p * tn + t
    for k in range(g):
        for i in range(tn):
            st_out[k * tn + i, :, 0:share] = st[k, :, i * share : (i + 1) * share]

    def st_copy(o, slot):
        return remote(
            st_out.at[o], st_in.at[slot], m_send.at[1], m_recv.at[1], zb + o // tn, lax.rem(o, tn)
        )

    @pl.loop(1, n)
    def _(d):
        st_copy(lax.rem(mine + d, n), mine).start()

    st_in[mine] = st_out[mine]
    pltpu.make_async_copy(
        st_in.at[pl.ds(0, n - 1)], st_in.at[pl.ds(0, n - 1)], m_recv.at[1]
    ).wait()
    got = st_in[...]
    tops = got[:, 0:1, 0:share]
    best = jnp.max(tops, axis=0)
    fall = tops - best[None]
    by = jnp.exp(fall)
    total = jnp.sum(got[:, 1:2, 0:share] * by, axis=0)
    spread = jnp.sum((got[:, 2:3, 0:share] + fall * got[:, 1:2, 0:share]) * by, axis=0)
    picked = jnp.sum(got[:, 3:4, 0:share], axis=0)
    weight = live[...].astype(jnp.float32)
    log_total = jnp.log(total)
    logp = (picked - best - log_total) * weight
    logprob[...] = logp
    entropy[...] = (log_total - spread / total) * weight

    member = lax.broadcasted_iota(jnp.int32, (seqs, share), 0) == seq_ids[...]
    s_sum = jnp.sum(jnp.where(member, logp, 0.0), axis=1, keepdims=True)
    s_live = jnp.sum(jnp.where(member, weight, 0.0), axis=1, keepdims=True)
    lanes = lax.broadcasted_iota(jnp.int32, (seqs, 128), 1)
    both = jnp.where(lanes < 64, s_sum, s_live)
    sq_seq_out[...] = both

    def seq_copy(d, slot):
        o = lax.rem(me + d, N)
        return remote(
            sq_seq_out, sq_seq_in.at[slot], m_send.at[2], m_recv.at[2], o // tn, lax.rem(o, tn)
        )

    @pl.loop(1, N)
    def _(d):
        seq_copy(d, me).start()

    sq_seq_in[me] = both
    pltpu.make_async_copy(
        sq_seq_in.at[pl.ds(0, N - 1)], sq_seq_in.at[pl.ds(0, N - 1)], m_recv.at[2]
    ).wait()
    sums_all = jnp.sum(sq_seq_in[...], axis=0)
    seq_mean[...] = sums_all[:, 0:1] / jnp.maximum(sums_all[:, 64:65], 1.0)

    pltpu.make_async_copy(sq_in.at[pl.ds(0, tn - 1)], sq_in.at[pl.ds(0, tn - 1)], m_send.at[0]).wait()
    pltpu.make_async_copy(st_in.at[pl.ds(0, n - 1)], st_in.at[pl.ds(0, n - 1)], m_send.at[1]).wait()
    pltpu.make_async_copy(
        sq_seq_in.at[pl.ds(0, N - 1)], sq_seq_in.at[pl.ds(0, N - 1)], m_send.at[2]
    ).wait()
    for d in range(1, g):
        tgt_copy(d, p).wait_send()
    for c in range(len(chunks)):
        for d in range(1, dp):
            w_copy(d, c, lax.rem(z + d, dp), z).wait_send()

    def sent(k, way):
        if way in (None, 0):

            @pl.when(p < g - 1)
            def _():
                z_copy(k, 0).wait_send()

        if way in (None, 1):

            @pl.when(p > 0)
            def _():
                z_copy(k, 1).wait_send()

    for s in range(g):
        each(s, sent)

    @pl.loop(0, g)
    def _(k):
        for j in range(chips):
            if j:
                p_copy(k, j, t).wait_send()
            s_copy(k, j, t ^ (2 * j)).wait_send()


def body(dp, tn, hidden, gain, head_weight, targets, seq_ids, live):
    g = GROUP if dp % GROUP == 0 else 1
    R, Dl = hidden.shape
    D = Dl * tn
    Kl, vocab_dev = head_weight.shape
    part, align, length = window(vocab_dev, g)
    chunks = pieces(length, align, max(1, length // 240))
    share = R // tn
    seqs = SEQ_DEV * dp
    N = dp * tn
    chips = tn // 2
    tile = max((n for n in range(128, 1025, 128) if R % n == 0), default=R)
    cfg = (dp, tn, g, part, align, length, chunks, tile)
    f32, dma = jnp.float32, pltpu.SemaphoreType.DMA
    vm = pl.BlockSpec(memory_space=pltpu.VMEM)
    nc = len(chunks)
    logprob, entropy, seq_mean = pl.pallas_call(
        functools.partial(kernel, cfg),
        out_shape=(
            jax.ShapeDtypeStruct((1, share), f32),
            jax.ShapeDtypeStruct((1, share), f32),
            jax.ShapeDtypeStruct((seqs, 1), f32),
        ),
        in_specs=[vm, vm, pl.BlockSpec(memory_space=pl.ANY), vm, vm, vm],
        out_specs=(vm, vm, vm),
        scratch_shapes=[
            pltpu.VMEM((g * R, D), jnp.bfloat16),
            pltpu.VMEM((length, D), jnp.bfloat16),
            pltpu.VMEM((g, 1, R), jnp.int32),
            pltpu.VMEM((8, R), f32),
            pltpu.VMEM((tn, 8, R), f32),
            pltpu.VMEM((g, 8, R), f32),
            pltpu.VMEM((g * tn, 8, 128), f32),
            pltpu.VMEM((g * tn, 8, 128), f32),
            pltpu.VMEM((seqs, 128), f32),
            pltpu.VMEM((N, seqs, 128), f32),
            dma((dp - 1, nc)), dma((dp - 1, nc)), dma((nc,)),
            dma((2, g)), dma((g,)),
            dma((g, chips)), dma((g, chips)),
            dma((g, chips)), dma((g, chips)),
            dma((max(g - 1, 1),)), dma((max(g - 1, 1),)),
            dma((3,)), dma((3,)),
        ],
        compiler_params=pltpu.CompilerParams(
            collective_id=0, has_side_effects=True, vmem_limit_bytes=60 * 2**20
        ),
        cost_estimate=pl.CostEstimate(
            flops=2 * g * R * length * D, bytes_accessed=2 * length * D, transcendentals=g * R * length
        ),
    )(
        hidden,
        gain.reshape(1, Dl),
        head_weight.T,
        targets.reshape(1, R),
        seq_ids.reshape(1, share),
        live.reshape(1, share),
    )
    return logprob.reshape(share), entropy.reshape(share), seq_mean.reshape(seqs)


def solution(mesh):
    placed = (
        P("dp", "tensor"),
        P("tensor"),
        P("dp", "tensor"),
        P("dp"),
        P(("dp", "tensor")),
        P(("dp", "tensor")),
    )
    return jax.shard_map(
        functools.partial(body, mesh.shape["dp"], mesh.shape["tensor"]),
        mesh=mesh,
        in_specs=placed,
        out_specs=(P(("dp", "tensor")), P(("dp", "tensor")), P()),
        check_vma=False,
    )
```

```python
import functools

import jax
import jax.numpy as jnp
from jax import lax
from jax.experimental import pallas as pl
from jax.experimental.pallas import tpu as pltpu
from jax.sharding import PartitionSpec as P

SEQ_DEV = 4
GROUP = 4
MESH = pl.DeviceIdType.MESH


def window(vocab_dev, group):
    part = vocab_dev // group
    for align in (16, 8):
        starts = [part * p // align * align for p in range(group)]
        need = max(part * (p + 1) - s for p, s in enumerate(starts))
        length = -(-need // align) * align
        if all(s + length <= vocab_dev for s in starts):
            return part, align, length
    raise ValueError("shard")


SHARES = (5, 7, 7, 7, 13, 13, 11)
WORK = ((0, 1, 2, 3), (4,), (5,), (6,))


def pieces(length, align):
    units, edges = length // align, [0]
    for i in range(len(SHARES)):
        edges.append(units * sum(SHARES[: i + 1]) // sum(SHARES))
    return [(a * align, (b - a) * align) for a, b in zip(edges, edges[1:])]


def kernel(
    cfg,
    hid, gain, wt, targets, seq_ids, live,
    logprob, entropy, seq_mean,
    x, w, tgt, sq_out, sq_in, st, st_out, st_in, sq_seq_out, sq_seq_in,
    w_send, w_recv, w_loc, z_send, z_recv, p_send, p_recv, s_send, s_recv, g_send, g_recv, m_send, m_recv,
):
    (dp, tn, g, part, align, length, chunks, tile) = cfg
    z, t = lax.axis_index("dp"), lax.axis_index("tensor")
    p = lax.rem(z, g)
    zb = z - p
    R, Dl = hid.shape
    Kl = wt.shape[1]
    chips = tn // 2
    N = dp * tn
    me = z * tn + t
    share = R // tn
    seqs = seq_mean.shape[0]

    def remote(src, dst, ss, rs, zz, tt):
        return pltpu.make_async_remote_copy(
            src_ref=src, dst_ref=dst, send_sem=ss, recv_sem=rs,
            device_id={"dp": zz, "tensor": tt}, device_id_type=MESH,
        )

    barrier = pltpu.get_barrier_semaphore()

    @pl.loop(1, N)
    def _(d):
        o = lax.rem(me + d, N)
        pl.semaphore_signal(
            barrier, inc=1, device_id={"dp": o // tn, "tensor": lax.rem(o, tn)}, device_id_type=MESH
        )

    pl.semaphore_wait(barrier, N - 1)

    def start_of(pp):
        return pl.multiple_of(part * pp // align * align, align)

    def w_copy(d, c, to, frm):
        off, size = chunks[c]
        return remote(
            wt.at[pl.ds(start_of(lax.rem(to, g)) + off, size)],
            w.at[pl.ds(off, size), pl.ds(pl.multiple_of(frm * Kl, Kl), Kl)],
            w_send.at[d - 1, c], w_recv.at[d - 1, c], to, t,
        )

    def w_own(c):
        off, size = chunks[c]
        return pltpu.make_async_copy(
            wt.at[pl.ds(start_of(p) + off, size)],
            w.at[pl.ds(off, size), pl.ds(pl.multiple_of(z * Kl, Kl), Kl)],
            w_loc.at[c],
        )

    def start_w(c):
        for d in range(1, dp):
            w_copy(d, c, lax.rem(z + d, dp), z).start()
        w_own(c).start()

    values = hid[...].astype(jnp.float32)
    sums = jnp.sum(values * values, axis=-1, keepdims=True)
    sq_out[...] = jnp.transpose(jnp.broadcast_to(sums, (R, 128)))[:8, :]

    def sq_copy(d, slot):
        return remote(sq_out, sq_in.at[slot], m_send.at[0], m_recv.at[0], z, lax.rem(t + d, tn))

    @pl.loop(1, tn)
    def _(d):
        sq_copy(d, t).start()

    sq_in[t] = sq_out[...]

    def tgt_copy(d, slot):
        return remote(
            targets, tgt.at[slot], g_send.at[d - 1], g_recv.at[d - 1], zb + lax.rem(p + d, g), t
        )

    for d in range(1, g):
        tgt_copy(d, p).start()
    tgt[p] = targets[...]
    start_w(0)
    pltpu.make_async_copy(
        sq_in.at[pl.ds(0, tn - 1)], sq_in.at[pl.ds(0, tn - 1)], m_recv.at[0]
    ).wait()
    squares = jnp.sum(sq_in[...], axis=0)
    wide = jnp.transpose(jnp.concatenate([squares] * 16, axis=0))
    scale = lax.rsqrt(wide / (tn * Dl) + 1e-05)
    rows0 = pl.ds(pl.multiple_of(p * R, R), R)
    for i in range(Dl // 128):
        cut = slice(i * 128, (i + 1) * 128)
        x[rows0, pl.ds(pl.multiple_of(t * Dl + i * 128, 128), 128)] = (
            values[:, cut] * scale * gain[:, cut].astype(jnp.float32)
        ).astype(jnp.bfloat16)

    def block(k, tt):
        return x.at[pl.ds(pl.multiple_of(k * R, R), R), pl.ds(pl.multiple_of(tt * Dl, Dl), Dl)]

    def z_copy(k, way):
        step = 1 if way == 0 else -1
        return remote(block(k, t), block(k, t), z_send.at[way, k], z_recv.at[k], z + step, t)

    def p_copy(k, j, src):
        return remote(
            block(k, src), block(k, src), p_send.at[k, j - 1], p_recv.at[k, j - 1], z, t ^ (2 * j)
        )

    def s_copy(k, j, src):
        return remote(block(k, src), block(k, src), s_send.at[k, j], s_recv.at[k, j], z, t ^ 1)

    square = chips == 4 and R % 32 == 0
    direct = (1, 2) if square else tuple(range(1, chips))

    def half_copy(k, h, src):
        at = block(k, src).at[pl.ds(h * (R // 2), R // 2)]
        return remote(at, at, p_send.at[k, 2 + h], p_recv.at[k, 2 + h], z, t ^ (4 if h == 0 else 2))

    def spread_out(k):
        for j in direct:
            p_copy(k, j, t).start()
        s_copy(k, 0, t).start()

    def gather_in(k):
        for j in direct:
            p_copy(k, j, t ^ (2 * j)).wait_recv()
            if square:
                half_copy(k, j - 1, t ^ (2 * j)).start()
            s_copy(k, j, t ^ (2 * j)).start()

    def gather_last(k):
        if square:
            for h in (0, 1):
                half_copy(k, h, t ^ 6).wait_recv()
            s_copy(k, 3, t ^ 6).start()

    def each(s, fn):
        if s == 0:
            fn(p, None)
            return

        @pl.when(p - s >= 0)
        def _():
            fn(p - s, 0)

        @pl.when(p + s < g)
        def _():
            fn(p + s, 1)

    def arrive(k, way):
        if way is not None:
            z_copy(k, way).wait_recv()
        if way in (None, 0):

            @pl.when(p < g - 1)
            def _():
                z_copy(k, 0).start()

        if way in (None, 1):

            @pl.when(p > 0)
            def _():
                z_copy(k, 1).start()

        spread_out(k)

    each(0, arrive)
    late = 1
    for s in range(1, g):
        start_w(late)
        late += 1
        each(s, arrive)
        each(s - 1, lambda k, way: gather_in(k))
    for c in range(late, len(chunks)):
        start_w(c)
    each(g - 1, lambda k, way: gather_in(k))
    for s in range(g):
        each(s, lambda k, way: gather_last(k))

    @pl.loop(0, g)
    def _(k):
        for j in range(chips):
            s_copy(k, j, t ^ 1 ^ (2 * j)).wait_recv()

    for d in range(1, g):
        tgt_copy(d, lax.rem(p - d + g, g)).wait_recv()

    first = t * (g * part) + start_of(p)
    low = p * part - start_of(p)
    for c, members in enumerate(WORK):
        for i in members:
            w_own(i).wait()
            for d in range(1, dp):
                w_copy(d, i, z, lax.rem(z - d + dp, dp)).wait_recv()
        off, size = chunks[members[0]][0], sum(chunks[i][1] for i in members)

        @pl.loop(0, R // tile * g)
        def _(b):
            k = b // (R // tile)
            lane = pl.multiple_of(lax.rem(b, R // tile) * tile, tile)
            scores = lax.dot_general(
                w[pl.ds(off, size), :],
                x[pl.ds(pl.multiple_of(b * tile, tile), tile), :],
                (((1,), (1,)), ((), ())),
                preferred_element_type=jnp.float32,
            )
            row = lax.broadcasted_iota(jnp.int32, (size, 1), 0) + off
            edge = c in (0, len(WORK) - 1)
            if edge:
                inside = (row >= low) & (row < low + part)
                top = jnp.max(jnp.where(inside, scores, -jnp.inf), axis=0, keepdims=True)
            else:
                top = jnp.max(scores, axis=0, keepdims=True)
            local = tgt[k, :, pl.ds(lane, tile)] - first
            local = jnp.where((local >= low) & (local < low + part), local, -1)
            picked = jnp.sum(jnp.where(row == local, scores, 0.0), axis=0, keepdims=True)
            if c > 0:
                was = st[k, 0:1, pl.ds(lane, tile)]
                top = jnp.maximum(top, was)
            shifted = scores - top
            if edge:
                shifted = jnp.where(inside, shifted, -1e4)
            expo = jnp.exp(shifted)
            total = jnp.sum(expo, axis=0, keepdims=True)
            spread = jnp.sum(expo * shifted, axis=0, keepdims=True)
            if c > 0:
                fall = was - top
                by = jnp.exp(fall)
                t0 = st[k, 1:2, pl.ds(lane, tile)]
                total += t0 * by
                spread += (st[k, 2:3, pl.ds(lane, tile)] + fall * t0) * by
                picked += st[k, 3:4, pl.ds(lane, tile)]
            st[k, 0:1, pl.ds(lane, tile)] = top
            st[k, 1:2, pl.ds(lane, tile)] = total
            st[k, 2:3, pl.ds(lane, tile)] = spread
            st[k, 3:4, pl.ds(lane, tile)] = picked

    n = g * tn
    mine = p * tn + t
    for k in range(g):
        for i in range(tn):
            st_out[k * tn + i, :, 0:share] = st[k, :, i * share : (i + 1) * share]

    def st_copy(o, slot):
        return remote(
            st_out.at[o], st_in.at[slot], m_send.at[1], m_recv.at[1], zb + o // tn, lax.rem(o, tn)
        )

    @pl.loop(1, n)
    def _(d):
        st_copy(lax.rem(mine + d, n), mine).start()

    st_in[mine] = st_out[mine]
    pltpu.make_async_copy(
        st_in.at[pl.ds(0, n - 1)], st_in.at[pl.ds(0, n - 1)], m_recv.at[1]
    ).wait()
    got = st_in[...]
    tops = got[:, 0:1, 0:share]
    best = jnp.max(tops, axis=0)
    fall = tops - best[None]
    by = jnp.exp(fall)
    total = jnp.sum(got[:, 1:2, 0:share] * by, axis=0)
    spread = jnp.sum((got[:, 2:3, 0:share] + fall * got[:, 1:2, 0:share]) * by, axis=0)
    picked = jnp.sum(got[:, 3:4, 0:share], axis=0)
    weight = live[...].astype(jnp.float32)
    log_total = jnp.log(total)
    logp = (picked - best - log_total) * weight
    logprob[...] = logp
    entropy[...] = (log_total - spread / total) * weight

    member = lax.broadcasted_iota(jnp.int32, (seqs, share), 0) == seq_ids[...]
    s_sum = jnp.sum(jnp.where(member, logp, 0.0), axis=1, keepdims=True)
    s_live = jnp.sum(jnp.where(member, weight, 0.0), axis=1, keepdims=True)
    lanes = lax.broadcasted_iota(jnp.int32, (seqs, 128), 1)
    both = jnp.where(lanes < 64, s_sum, s_live)
    sq_seq_out[...] = both

    def seq_copy(d, slot):
        o = lax.rem(me + d, N)
        return remote(
            sq_seq_out, sq_seq_in.at[slot], m_send.at[2], m_recv.at[2], o // tn, lax.rem(o, tn)
        )

    @pl.loop(1, N)
    def _(d):
        seq_copy(d, me).start()

    sq_seq_in[me] = both
    pltpu.make_async_copy(
        sq_seq_in.at[pl.ds(0, N - 1)], sq_seq_in.at[pl.ds(0, N - 1)], m_recv.at[2]
    ).wait()
    sums_all = jnp.sum(sq_seq_in[...], axis=0)
    seq_mean[...] = sums_all[:, 0:1] / jnp.maximum(sums_all[:, 64:65], 1.0)

    pltpu.make_async_copy(sq_in.at[pl.ds(0, tn - 1)], sq_in.at[pl.ds(0, tn - 1)], m_send.at[0]).wait()
    pltpu.make_async_copy(st_in.at[pl.ds(0, n - 1)], st_in.at[pl.ds(0, n - 1)], m_send.at[1]).wait()
    pltpu.make_async_copy(
        sq_seq_in.at[pl.ds(0, N - 1)], sq_seq_in.at[pl.ds(0, N - 1)], m_send.at[2]
    ).wait()
    for d in range(1, g):
        tgt_copy(d, p).wait_send()
    for c in range(len(chunks)):
        for d in range(1, dp):
            w_copy(d, c, lax.rem(z + d, dp), z).wait_send()

    def sent(k, way):
        if way in (None, 0):

            @pl.when(p < g - 1)
            def _():
                z_copy(k, 0).wait_send()

        if way in (None, 1):

            @pl.when(p > 0)
            def _():
                z_copy(k, 1).wait_send()

    for s in range(g):
        each(s, sent)

    @pl.loop(0, g)
    def _(k):
        for j in range(chips):
            s_copy(k, j, t ^ (2 * j)).wait_send()
        for j in direct:
            p_copy(k, j, t).wait_send()
            if square:
                half_copy(k, j - 1, t ^ (2 * j)).wait_send()


def body(dp, tn, hidden, gain, head_weight, targets, seq_ids, live):
    g = GROUP if dp % GROUP == 0 else 1
    R, Dl = hidden.shape
    D = Dl * tn
    Kl, vocab_dev = head_weight.shape
    part, align, length = window(vocab_dev, g)
    chunks = pieces(length, align)
    share = R // tn
    seqs = SEQ_DEV * dp
    N = dp * tn
    chips = tn // 2
    tile = max((n for n in range(128, 1025, 128) if R % n == 0), default=R)
    cfg = (dp, tn, g, part, align, length, chunks, tile)
    f32, dma = jnp.float32, pltpu.SemaphoreType.DMA
    vm = pl.BlockSpec(memory_space=pltpu.VMEM)
    nc = len(chunks)
    logprob, entropy, seq_mean = pl.pallas_call(
        functools.partial(kernel, cfg),
        out_shape=(
            jax.ShapeDtypeStruct((1, share), f32),
            jax.ShapeDtypeStruct((1, share), f32),
            jax.ShapeDtypeStruct((seqs, 1), f32),
        ),
        in_specs=[vm, vm, pl.BlockSpec(memory_space=pl.ANY), vm, vm, vm],
        out_specs=(vm, vm, vm),
        scratch_shapes=[
            pltpu.VMEM((g * R, D), jnp.bfloat16),
            pltpu.VMEM((length, D), jnp.bfloat16),
            pltpu.VMEM((g, 1, R), jnp.int32),
            pltpu.VMEM((8, R), f32),
            pltpu.VMEM((tn, 8, R), f32),
            pltpu.VMEM((g, 8, R), f32),
            pltpu.VMEM((g * tn, 8, 128), f32),
            pltpu.VMEM((g * tn, 8, 128), f32),
            pltpu.VMEM((seqs, 128), f32),
            pltpu.VMEM((N, seqs, 128), f32),
            dma((dp - 1, nc)), dma((dp - 1, nc)), dma((nc,)),
            dma((2, g)), dma((g,)),
            dma((g, max(chips, 4))), dma((g, max(chips, 4))),
            dma((g, chips)), dma((g, chips)),
            dma((max(g - 1, 1),)), dma((max(g - 1, 1),)),
            dma((3,)), dma((3,)),
        ],
        compiler_params=pltpu.CompilerParams(
            collective_id=0, has_side_effects=True, vmem_limit_bytes=60 * 2**20
        ),
        cost_estimate=pl.CostEstimate(
            flops=2 * g * R * length * D, bytes_accessed=2 * length * D, transcendentals=g * R * length
        ),
    )(
        hidden,
        gain.reshape(1, Dl),
        head_weight.T,
        targets.reshape(1, R),
        seq_ids.reshape(1, share),
        live.reshape(1, share),
    )
    return logprob.reshape(share), entropy.reshape(share), seq_mean.reshape(seqs)


def solution(mesh):
    placed = (
        P("dp", "tensor"),
        P("tensor"),
        P("dp", "tensor"),
        P("dp"),
        P(("dp", "tensor")),
        P(("dp", "tensor")),
    )
    return jax.shard_map(
        functools.partial(body, mesh.shape["dp"], mesh.shape["tensor"]),
        mesh=mesh,
        in_specs=placed,
        out_specs=(P(("dp", "tensor")), P(("dp", "tensor")), P()),
        check_vma=False,
    )
```
